512 devices in a mesh: gx: 32 (over x_hi, z, core), gy: 16 (over y, x_lo).
Axes of the slice: x: 4 (x_hi: 2, x_lo: 2; x = x_hi * 2 + x_lo), y: 8, z: 8, core: 2. Of those that a mesh axis runs over, the one named last changes fastest.
Arguments:
- iti: float32 [32, 16, 2, 512, 512], P('gx', 'gy'), may hold values from -3 to 3
- side: int32 [32, 16], P('gx', 'gy'), may hold values from 0 to 1, as said below
- owner: int32 [32, 16, 16], P('gx', 'gy'), may hold values from 0 to 15, each once within a row
Outputs:
- panels: float32 [32, 16, 2, 16, 24, 768], P('gx', 'gy')
The draws below stay inside these ranges and needn't reach their ends.
Inputs may be any that keep to these rules, and one draw needn't show every extreme that they name: `side`: boxes (i, j) and (i + 16, j) are the two siblings of one parent and have different sides. `owner`: for each box the owners of its panels are all different.
All inputs are finite; a program needn't handle non-finite values.
Results may differ from the reference program's by a relative error of at most 0.0003.
Values sent between devices are 32-bit elements; how exact they have to be, the bound alone decides.
A program may use at most 64 MiB of HBM per device.

```python
import math
import jax
import jax.numpy as jnp
from jax import lax

E = 128
SWEEPS = 15
BOX_COLS = 32
BOX_ROWS = 16
HALF_GX = 16
PANEL = 24


def draw_iti(key, part):
    shape = (BOX_COLS, BOX_ROWS, 2, 4 * E, 4 * E)
    spread = 0.665 / E ** 0.5
    values = jnp.clip(jax.random.normal(key, shape, jnp.float32) * spread, -4.0 * spread, 4.0 * spread)
    return values.astype(jnp.float32)


def draw_side(key, part):
    halves = jax.random.randint(key, (HALF_GX, BOX_ROWS), 0, 2, jnp.int32)
    return jnp.concatenate([halves, 1 - halves], axis=0).astype(jnp.int32)


def setup_inputs(seed: int = 0) -> dict:
    key_list = jax.random.split(jax.random.key(seed), 4)
    iti = draw_iti(jax.random.fold_in(key_list[3], 71), 0)
    side = draw_side(jax.random.fold_in(key_list[3], 71), 0)
    owner = jax.vmap(lambda own: jax.random.permutation(own, BOX_ROWS))(jax.random.split(key_list[2], BOX_COLS * BOX_ROWS)).reshape((BOX_COLS, BOX_ROWS, BOX_ROWS)).astype(jnp.int32)
    return dict(iti=iti, side=side, owner=owner)


def cprod(left, right):
    hp = lax.Precision.HIGHEST
    rr = jnp.dot(left[0], right[0], precision=hp, preferred_element_type=jnp.float32)
    ii = jnp.dot(left[1], right[1], precision=hp, preferred_element_type=jnp.float32)
    ri = jnp.dot(left[0], right[1], precision=hp, preferred_element_type=jnp.float32)
    ir = jnp.dot(left[1], right[0], precision=hp, preferred_element_type=jnp.float32)
    return jnp.stack([rr - ii, ri + ir])

def merge_one(ownmap, partner, east):
    ext = 3 * E
    p_ss = partner[:, :, ext:]
    p_se = partner[:, :, :ext]
    interface = cprod(p_ss, ownmap[:, ext:, ext:])
    own_cols = cprod(p_ss, ownmap[:, ext:, :ext])
    flag = east == 1
    start = jnp.where(flag, jnp.concatenate([p_se, own_cols], axis=-1), jnp.concatenate([own_cols, p_se], axis=-1))
    exterior = ownmap[:, :ext, :ext]
    zero = jnp.zeros_like(exterior)
    base = jnp.where(flag, jnp.concatenate([zero, exterior], axis=-1), jnp.concatenate([exterior, zero], axis=-1))
    total = start
    power = interface
    levels = (SWEEPS + 1).bit_length() - 1
    for level in range(levels):
        total = total + cprod(power, total)
        if level + 1 < levels:
            power = cprod(power, power)
    merged = (base + cprod(ownmap[:, :ext, ext:], total)) * math.sqrt(E)
    return merged

def reference(iti, side, owner):
    count = BOX_COLS * BOX_ROWS
    partner = jnp.roll(iti, HALF_GX, axis=0)[:, :, :, 3 * E:, :]
    merged = lax.map(lambda item: merge_one(item[0], item[1], item[2]), (iti.reshape(count, 2, 4 * E, 4 * E), partner.reshape(count, 2, E, 4 * E), side.reshape(count)))
    merged = merged.reshape(BOX_COLS, BOX_ROWS, 2, BOX_ROWS, PANEL, 6 * E)
    places = jnp.arange(BOX_ROWS, dtype=jnp.int32)
    match = (owner[:, :, :, None] == places[None, None, None, :]).astype(jnp.int32)
    inverse = lax.optimization_barrier(jnp.sum(places[None, None, :, None] * match, axis=2)).astype(jnp.int32)
    gathered = jnp.take_along_axis(merged, inverse[:, :, None, :, None, None], axis=3)
    return jnp.transpose(gathered, (0, 3, 2, 1, 4, 5))
```

```python
import functools
import math

import jax
import jax.numpy as jnp
from jax import lax
from jax.experimental import pallas as pl
from jax.experimental.pallas import tpu as pltpu
from jax.sharding import PartitionSpec as P

SWEEPS = 15
MESH = pl.DeviceIdType.MESH
f32, bf16 = jnp.float32, jnp.bfloat16


def split(x):
    high = x.astype(bf16)
    return high, (x - high.astype(f32)).astype(bf16)


def right_form(x):
    n = x.shape[1] // 2
    return jnp.concatenate([x, jnp.concatenate([-x[:, n:], x[:, :n]], axis=1)], axis=0)


def product(left, right):
    dot = functools.partial(jnp.dot, preferred_element_type=f32)
    return dot(left[0], right[0]) + (dot(left[0], right[1]) + dot(left[1], right[0]))


def both(x):
    high, low = split(x)
    return right_form(high), right_form(low)


def kernel(
    gx_size, ring, near,
    owner, side, iti, own_out, other_out, flag_out,
    box, qss, qse, left, left_high, left_low, own_send, other_send, flag_send, powers_high, powers_low, start,
    load_sem, edge_send, edge_recv, own_ssem, own_rsem, other_ssem, other_rsem, flag_ssem, flag_rsem, local_sem,
):
    edge = box.shape[-1] // 4
    ext = 3 * edge
    groups = ring * near
    rows = ext // groups
    weight = math.sqrt(edge)
    gx, gy = lax.axis_index("gx"), lax.axis_index("gy")
    y, x = gy // near, lax.rem(gy, near)
    sibling = (lax.rem(gx + gx_size // 2, gx_size), gy)
    half = ring // 2
    steps = [half]
    for s in range(half - 1, 0, -1):
        steps += [s, ring - s]
    places = [(s, t) for s in steps for t in range(near)] + [(0, t) for t in range(1, near)]
    peers = [lax.rem(y + s, ring) * near + lax.rem(x + t, near) for s, t in places]
    blocks = peers + [gy]
    n_peers = len(peers)

    loads = [
        pltpu.make_async_copy(iti.at[0, 0, :, ext:, :], box.at[:, ext:, :], load_sem.at[0]),
        pltpu.make_async_copy(iti.at[0, 0, :, :ext, :], box.at[:, :ext, :], load_sem.at[1]),
    ]
    for load in loads:
        load.start()
    barrier = pltpu.get_barrier_semaphore()
    pl.semaphore_signal(barrier, inc=1, device_id=sibling, device_id_type=MESH)
    for peer in peers:
        pl.semaphore_signal(barrier, inc=1, device_id=(gx, peer), device_id_type=MESH)
    flag_send[...] = jnp.full(flag_send.shape, side[0, 0].astype(f32))
    pl.semaphore_wait(barrier, n_peers + 1)

    ss = pltpu.make_async_remote_copy(
        iti.at[0, 0, :, ext:, ext:], qss, edge_send.at[0], edge_recv.at[0], device_id=sibling, device_id_type=MESH
    )
    se = pltpu.make_async_remote_copy(
        iti.at[0, 0, :, ext:, :ext], qse, edge_send.at[1], edge_recv.at[1], device_id=sibling, device_id_type=MESH
    )
    ss.start()
    se.start()
    flags = [
        pltpu.make_async_remote_copy(
            flag_send, flag_out.at[gy], flag_ssem.at[k], flag_rsem.at[k], device_id=(gx, peer), device_id_type=MESH
        )
        for k, peer in enumerate(peers)
    ]
    for flag in flags:
        flag.start()
    own_flag = pltpu.make_async_copy(flag_send, flag_out.at[gy], local_sem.at[0])
    own_flag.start()

    at = []
    for block in blocks:
        panel = jnp.int32(0)
        for p in range(groups):
            panel = jnp.maximum(panel, (owner[0, 0, p] == block).astype(jnp.int32) * p)
        at.append(panel * rows)
    for load in loads:
        load.wait()
    for k in range(groups):
        for c in range(2):
            left[k * rows:(k + 1) * rows, c * edge:(c + 1) * edge] = box[c, pl.ds(at[k], rows), ext:]
    high, low = split(left[...])
    left_high[...] = high
    left_low[...] = low
    edge_rows = [box[c, ext:, :] for c in range(2)]
    rss = both(jnp.concatenate([r[:, ext:] for r in edge_rows], axis=1))
    rse = both(jnp.concatenate([r[:, :ext] for r in edge_rows], axis=1))

    ss.wait_recv()
    q = split(jnp.concatenate([qss[0], qss[1]], axis=1))
    power = product(q, rss)
    total = product(q, rse)
    levels = (SWEEPS + 1).bit_length() - 1
    for level in range(levels):
        high, low = split(power)
        powers_high[level] = high
        powers_low[level] = low
        total = total + product((high, low), both(total))
        if level + 1 < levels:
            power = product((high, low), (right_form(high), right_form(low)))

    def send(total, base, buffer, out, ssem, rsem):
        factor = both(total)
        copies = []
        step = 4
        for g in range(0, groups, step):
            at_rows = slice(g * rows, (g + step) * rows)
            part = product((left_high[at_rows], left_low[at_rows]), factor)
            for k in range(g, g + step):
                for c in range(2):
                    piece = part[(k - g) * rows:(k - g + 1) * rows, c * ext:(c + 1) * ext]
                    if base:
                        piece = box[c, pl.ds(at[k], rows), :ext] + piece
                    buffer[k, c] = piece * weight
                if k < n_peers:
                    copy = pltpu.make_async_remote_copy(
                        buffer.at[k], out.at[:, gy], ssem.at[k], rsem.at[k],
                        device_id=(gx, peers[k]), device_id_type=MESH,
                    )
                else:
                    copy = pltpu.make_async_copy(buffer.at[k], out.at[:, gy], ssem.at[k])
                copy.start()
                copies.append(copy)
        return copies

    copies = send(total, True, own_send, own_out, own_ssem, own_rsem)
    se.wait_recv()
    total = jnp.concatenate([qse[0], qse[1]], axis=1)
    for level in range(levels):
        total = total + product((powers_high[level], powers_low[level]), both(total))
    copies += send(total, False, other_send, other_out, other_ssem, other_rsem)
    ss.wait_send()
    se.wait_send()
    own_flag.wait()
    for flag in flags:
        flag.wait()
    for copy in copies:
        copy.wait()


def on_device(ring, near, iti, side, owner):
    width = iti.shape[-1]
    edge = width // 4
    ext = 3 * edge
    groups = ring * near
    rows = ext // groups
    levels = (SWEEPS + 1).bit_length() - 1
    part = jax.ShapeDtypeStruct((2, groups, rows, ext), f32)
    dma = pltpu.SemaphoreType.DMA
    smem = pl.BlockSpec(memory_space=pltpu.SMEM)
    hbm = pl.BlockSpec(memory_space=pl.ANY)
    pinned = pl.BlockSpec(memory_space=pltpu.HBM)
    own, other, flags = pl.pallas_call(
        functools.partial(kernel, lax.axis_size("gx"), ring, near),
        out_shape=[part, part, jax.ShapeDtypeStruct((groups, 8, 128), f32)],
        in_specs=[smem, smem, pinned],
        out_specs=[hbm, hbm, hbm],
        scratch_shapes=[
            pltpu.VMEM((2, width, width), f32),
            pltpu.VMEM((2, edge, edge), f32),
            pltpu.VMEM((2, edge, ext), f32),
            pltpu.VMEM((ext, 2 * edge), f32),
            pltpu.VMEM((ext, 2 * edge), bf16),
            pltpu.VMEM((ext, 2 * edge), bf16),
            pltpu.VMEM((groups, 2, rows, ext), f32),
            pltpu.VMEM((groups, 2, rows, ext), f32),
            pltpu.VMEM((8, 128), f32),
            pltpu.VMEM((levels, edge, 2 * edge), bf16),
            pltpu.VMEM((levels, edge, 2 * edge), bf16),
            pltpu.VMEM((edge, 2 * ext), f32),
            dma((2,)), dma((2,)), dma((2,)),
            dma((groups,)), dma((groups,)), dma((groups,)), dma((groups,)), dma((groups,)), dma((groups,)),
            dma((1,)),
        ],
        compiler_params=pltpu.CompilerParams(
            collective_id=0, has_side_effects=True, vmem_limit_bytes=48 * 2**20
        ),
        name="merge",
    )(owner, side, iti)
    east = flags[:, 0, 0][None, :, None, None] == 1
    west_half = jnp.where(east, other, own)
    east_half = jnp.where(east, own, other)
    return jnp.concatenate([west_half, east_half], axis=-1)[None, None]


def solution(mesh):
    in_specs = (P("gx", "gy", None, None, None), P("gx", "gy"), P("gx", "gy", None))
    out_specs = P("gx", "gy", None, None, None, None)
    near = 2
    body = functools.partial(on_device, mesh.shape["gy"] // near, near)
    return jax.shard_map(body, mesh=mesh, in_specs=in_specs, out_specs=out_specs, check_vma=False)
```

```python
import functools
import math

import jax
import jax.numpy as jnp
from jax import lax
from jax.experimental import pallas as pl
from jax.experimental.pallas import tpu as pltpu
from jax.sharding import PartitionSpec as P

SWEEPS = 15
LEVELS = (SWEEPS + 1).bit_length() - 1
MESH = pl.DeviceIdType.MESH
f32, bf16 = jnp.float32, jnp.bfloat16
VMEM, HBM, SMEM = (pl.BlockSpec(memory_space=m) for m in (pltpu.VMEM, pltpu.HBM, pltpu.SMEM))
ANY = pl.BlockSpec(memory_space=pl.ANY)
DMA = pltpu.SemaphoreType.DMA


def split(x):
    high = x.astype(bf16)
    return high, (x - high.astype(f32)).astype(bf16)


def right_form(x):
    n = x.shape[1] // 2
    return jnp.concatenate([x, jnp.concatenate([-x[:, n:], x[:, :n]], axis=1)], axis=0)


def product(left, right):
    dot = functools.partial(jnp.dot, preferred_element_type=f32)
    return dot(left[0], right[0]) + (dot(left[0], right[1]) + dot(left[1], right[0]))


def both(x):
    high, low = split(x)
    return right_form(high), right_form(low)


def layout(ring, near):
    gy = lax.axis_index("gy")
    y, x = gy // near, lax.rem(gy, near)
    steps = [0]
    for s in range(1, ring // 2):
        steps += [s, ring - s]
    steps.append(ring // 2)
    places = [(s, t) for s in steps for t in range(near) if s or t]
    peers = [lax.rem(y + s, ring) * near + lax.rem(x + t, near) for s, t in places]
    senders = [lax.rem(y + ring - s, ring) * near + lax.rem(x + near - t, near) for s, t in places]
    return gy, peers, senders


def sibling_of(gx_size):
    return lax.rem(lax.axis_index("gx") + gx_size // 2, gx_size), lax.axis_index("gy")


def prepare(
    gx_size, ring, near,
    owner, side, iti,
    qss, edge_high, edge_low, ext_high, ext_low, left_high, left_low, base, flag,
    owner_s, box, left, load_sem, send_sem, recv_sem,
):
    edge = qss.shape[-1]
    ext = 3 * edge
    groups = ring * near
    rows = ext // groups
    loads = [
        pltpu.make_async_copy(owner, owner_s, load_sem.at[0]),
        pltpu.make_async_copy(iti.at[0, 0, :, ext:, :], box.at[:, ext:, :], load_sem.at[1]),
        pltpu.make_async_copy(iti.at[0, 0, :, :ext, :], box.at[:, :ext, :], load_sem.at[2]),
    ]
    sibling = sibling_of(gx_size)
    barrier = pltpu.get_barrier_semaphore()
    pl.semaphore_signal(barrier, inc=1, device_id=sibling, device_id_type=MESH)
    for load in loads:
        load.start()
    pl.semaphore_wait(barrier, 1)
    copy = pltpu.make_async_remote_copy(
        iti.at[0, 0, :, ext:, ext:], qss, send_sem, recv_sem, device_id=sibling, device_id_type=MESH
    )
    copy.start()

    for load in loads:
        load.wait()
    edge_rows = [box[c, ext:, :] for c in range(2)]
    edge_high[...], edge_low[...] = both(jnp.concatenate([r[:, ext:] for r in edge_rows], axis=1))
    ext_high[...], ext_low[...] = both(jnp.concatenate([r[:, :ext] for r in edge_rows], axis=1))
    flag[...] = jnp.full(flag.shape, side[0, 0].astype(f32))
    gy, peers, _ = layout(ring, near)
    owners = [owner_s[0, 0, p] for p in range(groups)]
    for k, block in enumerate(peers + [gy]):
        panel = jnp.int32(0)
        for p in range(1, groups):
            panel = jnp.maximum(panel, (owners[p] == block).astype(jnp.int32) * p)
        for c in range(2):
            found = box[c, pl.ds(panel * rows, rows), :]
            left[k * rows:(k + 1) * rows, c * edge:(c + 1) * edge] = found[:, ext:]
            base[k, c] = found[:, :ext] * math.sqrt(edge)
    left_high[...], left_low[...] = split(left[...])
    copy.wait()


def merge(
    gx_size, ring, near,
    iti, qss, edge_high, edge_low, ext_high, ext_low, left_high, left_low, base, flag,
    out,
    qse, own_send, other_send, own_in, other_in, flag_in, powers_high, powers_low,
    edge_ssem, edge_rsem, own_ssem, own_rsem, other_ssem, other_rsem, flag_ssem, flag_rsem,
):
    edge = qss.shape[-1]
    ext = 3 * edge
    groups = ring * near
    rows = ext // groups
    weight = math.sqrt(edge)
    gx = lax.axis_index("gx")
    gy, peers, senders = layout(ring, near)
    sibling = sibling_of(gx_size)
    n_peers = len(peers)

    barrier = pltpu.get_barrier_semaphore()
    for peer in reversed(peers):
        pl.semaphore_signal(barrier, inc=1, device_id=(gx, peer), device_id_type=MESH)
    pl.semaphore_signal(barrier, inc=1, device_id=sibling, device_id_type=MESH)

    q = split(jnp.concatenate([qss[0], qss[1]], axis=1))
    power = product(q, (edge_high[...], edge_low[...]))
    total = product(q, (ext_high[...], ext_low[...]))
    for level in range(LEVELS):
        high, low = split(power)
        powers_high[level] = high
        powers_low[level] = low
        total = total + product((high, low), both(total))
        if level + 1 < LEVELS:
            power = product((high, low), (right_form(high), right_form(low)))

    step = 4

    def compute(total, add, buffer):
        factor = both(total)

        def part(g):
            at_rows = slice(g * rows, (g + step) * rows)
            value = product((left_high[at_rows], left_low[at_rows]), factor) * weight
            for k in range(g, g + step):
                for c in range(2):
                    piece = value[(k - g) * rows:(k - g + 1) * rows, c * ext:(c + 1) * ext]
                    buffer[k, c] = base[k, c] + piece if add else piece

        return part

    def send(g, buffer, into, ssem, rsem):
        copies = []
        for k in range(g, min(g + step, n_peers)):
            copy = pltpu.make_async_remote_copy(
                buffer.at[k], into.at[k], ssem.at[k], rsem.at[k], device_id=(gx, peers[k]), device_id_type=MESH
            )
            copy.start()
            copies.append(copy)
        return copies

    own = compute(total, True, own_send)
    own(0)
    pl.semaphore_wait(barrier, n_peers + 1)
    own_copies = send(0, own_send, own_in, own_ssem, own_rsem)
    se = pltpu.make_async_remote_copy(
        iti.at[0, 0, :, ext:, :ext], qse, edge_ssem, edge_rsem, device_id=sibling, device_id_type=MESH
    )
    se.start()
    for g in range(step, groups, step):
        own(g)
        own_copies += send(g, own_send, own_in, own_ssem, own_rsem)
    flags = [
        pltpu.make_async_remote_copy(
            flag, flag_in.at[k], flag_ssem.at[k], flag_rsem.at[k], device_id=(gx, peer), device_id_type=MESH
        )
        for k, peer in enumerate(peers)
    ]
    for copy in flags:
        copy.start()
    se.wait()
    total = jnp.concatenate([qse[0], qse[1]], axis=1)
    for level in range(LEVELS):
        total = total + product((powers_high[level], powers_low[level]), both(total))
    other = compute(total, False, other_send)
    other_copies = []
    for g in range(0, groups, step):
        other(g)
        other_copies += send(g, other_send, other_in, other_ssem, other_rsem)

    def arrange(own_part, other_part, east, sender):
        for c in range(2):
            east_rows = jnp.broadcast_to(east[:1, :1], (rows, ext)) == 1
            a, b = own_part[c], other_part[c]
            out[c, sender, :, :ext] = jnp.where(east_rows, b, a)
            out[c, sender, :, ext:] = jnp.where(east_rows, a, b)

    arrange(own_send.at[n_peers], other_send.at[n_peers], flag[...], gy)
    for k in range(n_peers):
        flags[k].wait()
        own_copies[k].wait()
        other_copies[k].wait()
        arrange(own_in.at[k], other_in.at[k], flag_in[k], senders[k])


def write(arranged, out, sem):
    parts, groups = arranged.shape[:2]
    copies = [
        pltpu.make_async_copy(arranged.at[c, g], out.at[0, 0, c, g], sem.at[c, g])
        for c in range(parts) for g in range(groups)
    ]
    for copy in copies:
        copy.start()
    for copy in copies:
        copy.wait()


def on_device(gx_size, ring, near, iti, side, owner):
    width = iti.shape[-1]
    edge = width // 4
    ext = 3 * edge
    groups = ring * near
    rows = ext // groups
    shape = jax.ShapeDtypeStruct
    params = functools.partial(pltpu.CompilerParams, has_side_effects=True, vmem_limit_bytes=40 * 2**20)
    iti, owner = (pltpu.with_memory_space_constraint(a, pltpu.HBM) for a in (iti, owner))
    prepared = pl.pallas_call(
        functools.partial(prepare, gx_size, ring, near),
        out_shape=[
            shape((2, edge, edge), f32),
            shape((2 * edge, 2 * edge), bf16), shape((2 * edge, 2 * edge), bf16),
            shape((2 * edge, 2 * ext), bf16), shape((2 * edge, 2 * ext), bf16),
            shape((ext, 2 * edge), bf16), shape((ext, 2 * edge), bf16),
            shape((groups, 2, rows, ext), f32),
            shape((1, 128), f32),
        ],
        in_specs=[HBM, SMEM, HBM],
        out_specs=[VMEM] * 9,
        scratch_shapes=[
            pltpu.SMEM((1, 1, groups), jnp.int32),
            pltpu.VMEM((2, width, width), f32), pltpu.VMEM((ext, 2 * edge), f32),
            DMA((3,)), DMA, DMA,
        ],
        compiler_params=params(collective_id=0),
        name="prepare",
    )(owner, side, iti)
    arranged = pl.pallas_call(
        functools.partial(merge, gx_size, ring, near),
        out_shape=shape((2, groups, rows, 2 * ext), f32),
        in_specs=[HBM] + [VMEM] * 9,
        out_specs=VMEM,
        scratch_shapes=[
            pltpu.VMEM((2, edge, ext), f32),
            *[pltpu.VMEM((groups, 2, rows, ext), f32)] * 4,
            pltpu.VMEM((groups, 1, 128), f32),
            *[pltpu.VMEM((LEVELS, edge, 2 * edge), bf16)] * 2,
            DMA, DMA, *[DMA((groups,))] * 6,
        ],
        compiler_params=params(collective_id=1),
        name="merge",
    )(iti, *prepared)
    arranged = pltpu.with_memory_space_constraint(arranged, pltpu.VMEM)
    return pl.pallas_call(
        write,
        out_shape=shape((1, 1, 2, groups, rows, 2 * ext), f32),
        in_specs=[VMEM],
        out_specs=ANY,
        scratch_shapes=[DMA((2, groups))],
        name="write",
    )(arranged)


def solution(mesh):
    in_specs = (P("gx", "gy", None, None, None), P("gx", "gy"), P("gx", "gy", None))
    out_specs = P("gx", "gy", None, None, None, None)
    near = 2
    body = functools.partial(on_device, mesh.shape["gx"], mesh.shape["gy"] // near, near)
    return jax.shard_map(body, mesh=mesh, in_specs=in_specs, out_specs=out_specs, check_vma=False)
```

```python
import functools
import math

import jax
import jax.numpy as jnp
from jax import lax
from jax.experimental import pallas as pl
from jax.experimental.pallas import tpu as pltpu
from jax.sharding import PartitionSpec as P

SWEEPS = 15
LEVELS = (SWEEPS + 1).bit_length() - 1
MESH = pl.DeviceIdType.MESH
EARLY, LATE = (2, 1, 0), (3,)
f32, bf16 = jnp.float32, jnp.bfloat16
VMEM, HBM, SMEM = (pl.BlockSpec(memory_space=m) for m in (pltpu.VMEM, pltpu.HBM, pltpu.SMEM))
DMA = pltpu.SemaphoreType.DMA


def split(x):
    high = x.astype(bf16)
    return high, (x - high.astype(f32)).astype(bf16)


def right_form(x):
    n = x.shape[1] // 2
    return jnp.concatenate([x, jnp.concatenate([-x[:, n:], x[:, :n]], axis=1)], axis=0)


def product(left, right):
    dot = functools.partial(jnp.dot, preferred_element_type=f32)
    return dot(left[0], right[0]) + (dot(left[0], right[1]) + dot(left[1], right[0]))


def both(x):
    high, low = split(x)
    return right_form(high), right_form(low)


def layout(ring, near):
    gy = lax.axis_index("gy")
    y, x = gy // near, lax.rem(gy, near)

    def index(s, t):
        return lax.rem(y + s + ring, ring) * near + lax.rem(x + t + near, near)

    half = ring // 2
    ahead = [(s, t) for s in range(1, half) for t in range(near)] + [(half, 0)]
    behind = [(-s, t) for s in range(1, half) for t in range(near)] + [(-half, 1)]
    places = ahead + [(0, 1)] + behind
    peers = [index(s, t) for s, t in places]
    senders = [index(-s, -t) for s, t in places]
    onward = [index(s - 1, t) for s, t in ahead] + [None] + [index(s + 1, t) for s, t in behind]
    return gy, peers, senders, onward, (index(1, 0), index(-1, 0)), len(ahead)


def sibling_of(gx_size):
    return lax.rem(lax.axis_index("gx") + gx_size // 2, gx_size), lax.axis_index("gy")


def kernel(
    gx_size, ring, near,
    owner, side, iti,
    out,
    owner_s, columns, edge_box, ext_box, left, qss, qse, edge_high, edge_low, ext_high, ext_low, left_high, left_low, base, flag, near_left,
    own_send, other_send, own_in, other_in, flag_in, powers_high, powers_low, solved, solved_in,
    load_sem, send_sem, recv_sem, near_ssem, near_rsem, edge_ssem, edge_rsem, solved_ssem, solved_rsem,
    own_ssem, own_rsem, other_ssem, other_rsem, flag_ssem, flag_rsem,
):
    edge = qss.shape[-1]
    ext = 3 * edge
    groups = ring * near
    rows = ext // groups
    loads = [
        pltpu.make_async_copy(owner, owner_s, load_sem.at[0]),
        pltpu.make_async_copy(iti.at[0, 0, :, :ext, ext:], columns, load_sem.at[1]),
        pltpu.make_async_copy(iti.at[0, 0, :, ext:, :], edge_box, load_sem.at[2]),
        pltpu.make_async_copy(iti.at[0, 0, :, :ext, :ext], ext_box, load_sem.at[3]),
    ]
    for load in loads:
        load.start()
    sibling = sibling_of(gx_size)
    gx = lax.axis_index("gx")
    gy, peers, senders, onward, neighbours, n_ahead = layout(ring, near)
    n_peers = len(peers)
    weight = math.sqrt(edge)
    barrier = pltpu.get_barrier_semaphore()
    pl.semaphore_signal(barrier, inc=1, device_id=sibling, device_id_type=MESH)
    for peer in reversed(peers):
        pl.semaphore_signal(barrier, inc=1, device_id=(gx, peer), device_id_type=MESH)
    pl.semaphore_wait(barrier, n_peers + 1)
    copy = pltpu.make_async_remote_copy(
        iti.at[0, 0, :, ext:, ext:], qss, send_sem, recv_sem, device_id=sibling, device_id_type=MESH
    )
    copy.start()

    loads[0].wait()
    loads[1].wait()
    owners = [owner_s[0, 0, p] for p in range(groups)]
    at = []
    for k, block in enumerate(peers + [gy]):
        panel = jnp.int32(0)
        for p in range(1, groups):
            panel = jnp.maximum(panel, (owners[p] == block).astype(jnp.int32) * p)
        at.append(panel * rows)
        for c in range(2):
            left[k * rows:(k + 1) * rows, c * edge:(c + 1) * edge] = columns[c, pl.ds(at[k], rows), :]
    span = n_ahead * rows
    near_copies = [
        pltpu.make_async_remote_copy(
            left.at[g * ext // 2:g * ext // 2 + span], near_left.at[g], near_ssem.at[g], near_rsem.at[g],
            device_id=(gx, neighbour), device_id_type=MESH,
        )
        for g, neighbour in enumerate(neighbours)
    ]
    for near_copy in near_copies:
        near_copy.start()
    left_high[...], left_low[...] = split(left[...])
    loads[2].wait()
    edge_rows = [edge_box[c] for c in range(2)]
    edge_high[...], edge_low[...] = both(jnp.concatenate([r[:, ext:] for r in edge_rows], axis=1))
    ext_high[...], ext_low[...] = both(jnp.concatenate([r[:, :ext] for r in edge_rows], axis=1))
    flag[...] = jnp.full(flag.shape, side[0, 0].astype(f32))
    loads[3].wait()
    for k in range(groups):
        for c in range(2):
            base[k, c] = ext_box[c, pl.ds(at[k], rows), :] * math.sqrt(edge)
    copy.wait()
    se = pltpu.make_async_remote_copy(
        iti.at[0, 0, :, ext:, :ext], qse, edge_ssem, edge_rsem, device_id=sibling, device_id_type=MESH
    )
    se.start()
    q = split(jnp.concatenate([qss[0], qss[1]], axis=1))
    power = product(q, (edge_high[...], edge_low[...]))
    total = product(q, (ext_high[...], ext_low[...]))
    for level in range(LEVELS):
        high, low = split(power)
        powers_high[level] = high
        powers_low[level] = low
        total = total + product((high, low), both(total))
        if level + 1 < LEVELS:
            power = product((high, low), (right_form(high), right_form(low)))

    def panels(value, buffer, first, add=False):
        for m in range(value.shape[0] // rows):
            for c in range(2):
                piece = value[m * rows:(m + 1) * rows, c * ext:(c + 1) * ext]
                buffer[first + m, c] = base[first + m, c] + piece if add else piece

    def send(k, buffer, into, ssem, rsem, peer):
        copy = pltpu.make_async_remote_copy(
            buffer.at[k], into.at[k], ssem.at[k], rsem.at[k], device_id=(gx, peer), device_id_type=MESH
        )
        copy.start()
        return copy

    own_copies = {}
    factor = both(total)

    pair = [[2 * s, 2 * s + 1, 2 * s + groups // 2, 2 * s + 1 + groups // 2] for s in range(4)]

    def own(s):
        for k in pair[s][::2]:
            at_rows = slice(k * rows, (k + 2) * rows)
            panels(product((left_high[at_rows], left_low[at_rows]), factor) * weight, own_send, k, add=True)

    def send_own(s):
        for k in (pair[s][0], pair[s][2], pair[s][1], pair[s][3]):
            if k < n_peers:
                own_copies[k] = send(k, own_send, own_in, own_ssem, own_rsem, peers[k])

    for s in EARLY:
        own(s)
        send_own(s)
    for s in LATE:
        own(s)
    flags = [
        pltpu.make_async_remote_copy(
            flag, flag_in.at[k], flag_ssem.at[k], flag_rsem.at[k], device_id=(gx, peer), device_id_type=MESH
        )
        for k, peer in enumerate(peers)
    ]
    se.wait()
    total = jnp.concatenate([qse[0], qse[1]], axis=1)
    for level in range(LEVELS):
        total = total + product((powers_high[level], powers_low[level]), both(total))
    solved[...] = total
    solved_copies = [
        pltpu.make_async_remote_copy(
            solved, solved_in.at[g], solved_ssem.at[g], solved_rsem.at[g], device_id=(gx, neighbour), device_id_type=MESH
        )
        for g, neighbour in enumerate(neighbours)
    ]
    for copy in solved_copies:
        copy.start()
    for s in LATE:
        send_own(s)
    for copy in flags:
        copy.start()
    other_copies = {}
    for k in (n_ahead, n_peers):
        at_rows = slice((k // 2) * 2 * rows, (k // 2) * 2 * rows + 2 * rows)
        value = product((left_high[at_rows], left_low[at_rows]), both(total)) * weight
        panels(value[(k % 2) * rows:(k % 2 + 1) * rows], other_send, k)
        if k < n_peers:
            other_copies[k] = send(k, other_send, other_in, other_ssem, other_rsem, peers[k])
    for g in range(2):
        first = g * groups // 2
        near_copies[g].wait()
        solved_copies[g].wait()
        value = product(split(near_left[g]), both(solved_in[g])) * weight
        panels(value[:rows], other_in, first)
        panels(value[rows:], other_send, first + 1)
        for k in reversed(range(first + 1, first + n_ahead)):
            other_copies[k] = send(k, other_send, other_in, other_ssem, other_rsem, onward[k])

    def arrange(own_part, other_part, east, sender):
        for c in range(2):
            east_rows = jnp.broadcast_to(east[:1, :1], (rows, ext)) == 1
            a, b = own_part[c], other_part[c]
            out[c, sender, :, :ext] = jnp.where(east_rows, b, a)
            out[c, sender, :, ext:] = jnp.where(east_rows, a, b)

    arrange(own_send.at[n_peers], other_send.at[n_peers], flag[...], gy)
    for k in range(n_peers):
        flags[k].wait()
        own_copies[k].wait()
        if k in other_copies:
            other_copies[k].wait()
        arrange(own_in.at[k], other_in.at[k], flag_in[k], senders[k])


def on_device(gx_size, ring, near, iti, side, owner):
    width = iti.shape[-1]
    edge = width // 4
    ext = 3 * edge
    groups = ring * near
    rows = ext // groups
    span = (groups - near) // 2 * rows
    vmem, sems = pltpu.VMEM, DMA((groups,))
    iti, owner = (pltpu.with_memory_space_constraint(a, pltpu.HBM) for a in (iti, owner))
    out = pl.pallas_call(
        functools.partial(kernel, gx_size, ring, near),
        out_shape=jax.ShapeDtypeStruct((2, groups, rows, 2 * ext), f32),
        in_specs=[HBM, SMEM, HBM],
        out_specs=VMEM,
        scratch_shapes=[
            pltpu.SMEM((1, 1, groups), jnp.int32), vmem((2, ext, edge), f32), vmem((2, edge, width), f32),
            vmem((2, ext, ext), f32), vmem((ext, 2 * edge), f32),
            vmem((2, edge, edge), f32), vmem((2, edge, ext), f32),
            *[vmem((2 * edge, 2 * edge), bf16)] * 2, *[vmem((2 * edge, 2 * ext), bf16)] * 2,
            *[vmem((ext, 2 * edge), bf16)] * 2, vmem((groups, 2, rows, ext), f32), vmem((1, 128), f32),
            vmem((2, span, 2 * edge), f32),
            *[vmem((groups, 2, rows, ext), f32)] * 4, vmem((groups, 1, 128), f32),
            *[vmem((LEVELS, edge, 2 * edge), bf16)] * 2, vmem((edge, 2 * ext), f32), vmem((2, edge, 2 * ext), f32),
            DMA((4,)), DMA, DMA, DMA((2,)), DMA((2,)), DMA, DMA, DMA((2,)), DMA((2,)), *[sems] * 6,
        ],
        compiler_params=pltpu.CompilerParams(
            collective_id=0, has_side_effects=True, vmem_limit_bytes=40 * 2**20
        ),
        name="merge",
    )(owner, side, iti)
    return out[None, None]


def solution(mesh):
    in_specs = (P("gx", "gy", None, None, None), P("gx", "gy"), P("gx", "gy", None))
    out_specs = P("gx", "gy", None, None, None, None)
    near = 2
    body = functools.partial(on_device, mesh.shape["gx"], mesh.shape["gy"] // near, near)
    return jax.shard_map(body, mesh=mesh, in_specs=in_specs, out_specs=out_specs, check_vma=False)
```

```python
import functools
import math

import jax
import jax.numpy as jnp
from jax import lax
from jax.experimental import pallas as pl
from jax.experimental.pallas import tpu as pltpu
from jax.sharding import PartitionSpec as P

SWEEPS = 15
LEVELS = (SWEEPS + 1).bit_length() - 1
MESH = pl.DeviceIdType.MESH
EARLY, LATE = (2, 1), (0, 3)
f32, bf16 = jnp.float32, jnp.bfloat16
VMEM, HBM, SMEM = (pl.BlockSpec(memory_space=m) for m in (pltpu.VMEM, pltpu.HBM, pltpu.SMEM))
DMA = pltpu.SemaphoreType.DMA


def split(x):
    high = x.astype(bf16)
    return high, (x - high.astype(f32)).astype(bf16)


def right_form(x):
    n = x.shape[1] // 2
    return jnp.concatenate([x, jnp.concatenate([-x[:, n:], x[:, :n]], axis=1)], axis=0)


def product(left, right):
    dot = functools.partial(jnp.dot, preferred_element_type=f32)
    return dot(left[0], right[0]) + (dot(left[0], right[1]) + dot(left[1], right[0]))


def both(x):
    high, low = split(x)
    return right_form(high), right_form(low)


def layout(ring, near):
    gy = lax.axis_index("gy")
    y, x = gy // near, lax.rem(gy, near)

    def index(s, t):
        return lax.rem(y + s + ring, ring) * near + lax.rem(x + t + near, near)

    half = ring // 2
    ahead = [(s, t) for s in range(1, half) for t in range(near)] + [(half, 0)]
    behind = [(-s, t) for s in range(1, half) for t in range(near)] + [(-half, 1)]
    places = ahead + [(0, 1)] + behind
    peers = [index(s, t) for s, t in places]
    senders = [index(-s, -t) for s, t in places]
    onward = [index(s - 1, t) for s, t in ahead] + [None] + [index(s + 1, t) for s, t in behind]
    return gy, peers, senders, onward, (index(1, 0), index(-1, 0)), len(ahead)


def sibling_of(gx_size):
    return lax.rem(lax.axis_index("gx") + gx_size // 2, gx_size), lax.axis_index("gy")


def kernel(
    gx_size, ring, near,
    owner, side, iti,
    out,
    owner_s, columns, edge_box, ext_box, left, qss, qse, edge_high, edge_low, ext_high, ext_low, left_high, left_low, flag, near_left,
    own_send, other_send, own_in, other_in, flag_in, powers_high, powers_low, solved, solved_in,
    load_sem, send_sem, recv_sem, near_ssem, near_rsem, edge_ssem, edge_rsem, solved_ssem, solved_rsem,
    own_ssem, own_rsem, other_ssem, other_rsem, flag_ssem, flag_rsem,
):
    edge = qss.shape[-1]
    ext = 3 * edge
    groups = ring * near
    rows = ext // groups
    loads = [
        pltpu.make_async_copy(owner, owner_s, load_sem.at[0]),
        pltpu.make_async_copy(iti.at[0, 0, :, :ext, ext:], columns, load_sem.at[1]),
        pltpu.make_async_copy(iti.at[0, 0, :, ext:, :], edge_box, load_sem.at[2]),
        pltpu.make_async_copy(iti.at[0, 0, :, :ext, :ext], ext_box, load_sem.at[3]),
    ]
    for load in loads:
        load.start()
    sibling = sibling_of(gx_size)
    gx = lax.axis_index("gx")
    gy, peers, senders, onward, neighbours, n_ahead = layout(ring, near)
    n_peers = len(peers)
    weight = math.sqrt(edge)
    barrier = pltpu.get_barrier_semaphore()
    pl.semaphore_signal(barrier, inc=1, device_id=sibling, device_id_type=MESH)
    for peer in reversed(peers):
        pl.semaphore_signal(barrier, inc=1, device_id=(gx, peer), device_id_type=MESH)
    pl.semaphore_wait(barrier, n_peers + 1)
    copy = pltpu.make_async_remote_copy(
        iti.at[0, 0, :, ext:, ext:], qss, send_sem, recv_sem, device_id=sibling, device_id_type=MESH
    )
    copy.start()

    loads[0].wait()
    loads[1].wait()
    owners = [owner_s[0, 0, p] for p in range(groups)]
    at = []
    for k, block in enumerate(peers + [gy]):
        panel = jnp.int32(0)
        for p in range(1, groups):
            panel = jnp.maximum(panel, (owners[p] == block).astype(jnp.int32) * p)
        at.append(panel * rows)
        for c in range(2):
            left[k * rows:(k + 1) * rows, c * edge:(c + 1) * edge] = columns[c, pl.ds(at[k], rows), :]
    span = n_ahead * rows
    near_copies = [
        pltpu.make_async_remote_copy(
            left.at[g * ext // 2:g * ext // 2 + span], near_left.at[g], near_ssem.at[g], near_rsem.at[g],
            device_id=(gx, neighbour), device_id_type=MESH,
        )
        for g, neighbour in enumerate(neighbours)
    ]
    for near_copy in near_copies:
        near_copy.start()
    left_high[...], left_low[...] = split(left[...])
    loads[2].wait()
    edge_rows = [edge_box[c] for c in range(2)]
    edge_high[...], edge_low[...] = both(jnp.concatenate([r[:, ext:] for r in edge_rows], axis=1))
    ext_high[...], ext_low[...] = both(jnp.concatenate([r[:, :ext] for r in edge_rows], axis=1))
    flag[...] = jnp.full(flag.shape, side[0, 0].astype(f32))
    copy.wait()
    se = pltpu.make_async_remote_copy(
        iti.at[0, 0, :, ext:, :ext], qse, edge_ssem, edge_rsem, device_id=sibling, device_id_type=MESH
    )
    se.start()
    q = split(jnp.concatenate([qss[0], qss[1]], axis=1))
    power = product(q, (edge_high[...], edge_low[...]))
    total = product(q, (ext_high[...], ext_low[...]))
    for level in range(LEVELS):
        high, low = split(power)
        powers_high[level] = high
        powers_low[level] = low
        total = total + product((high, low), both(total))
        if level + 1 < LEVELS:
            power = product((high, low), (right_form(high), right_form(low)))

    def panels(value, buffer, first, add=False):
        for m in range(value.shape[0] // rows):
            for c in range(2):
                piece = value[m * rows:(m + 1) * rows, c * ext:(c + 1) * ext]
                if add:
                    piece = ext_box[c, pl.ds(at[first + m], rows), :] * weight + piece
                buffer[first + m, c] = piece

    def send(k, buffer, into, ssem, rsem, peer):
        copy = pltpu.make_async_remote_copy(
            buffer.at[k], into.at[k], ssem.at[k], rsem.at[k], device_id=(gx, peer), device_id_type=MESH
        )
        copy.start()
        return copy

    own_copies = {}
    factor = both(total)

    pair = [[2 * s, 2 * s + 1, 2 * s + groups // 2, 2 * s + 1 + groups // 2] for s in range(4)]

    def own(s):
        for k in pair[s][::2]:
            at_rows = slice(k * rows, (k + 2) * rows)
            panels(product((left_high[at_rows], left_low[at_rows]), factor) * weight, own_send, k, add=True)

    def send_own(s):
        for k in (pair[s][0], pair[s][2], pair[s][1], pair[s][3]):
            if k < n_peers:
                own_copies[k] = send(k, own_send, own_in, own_ssem, own_rsem, peers[k])

    loads[3].wait()
    for s in EARLY:
        own(s)
        send_own(s)
    for s in LATE:
        own(s)
    flags = [
        pltpu.make_async_remote_copy(
            flag, flag_in.at[k], flag_ssem.at[k], flag_rsem.at[k], device_id=(gx, peer), device_id_type=MESH
        )
        for k, peer in enumerate(peers)
    ]
    se.wait()
    total = jnp.concatenate([qse[0], qse[1]], axis=1)
    for level in range(LEVELS):
        total = total + product((powers_high[level], powers_low[level]), both(total))
    solved[...] = total
    solved_copies = [
        pltpu.make_async_remote_copy(
            solved, solved_in.at[g], solved_ssem.at[g], solved_rsem.at[g], device_id=(gx, neighbour), device_id_type=MESH
        )
        for g, neighbour in enumerate(neighbours)
    ]
    for copy in solved_copies:
        copy.start()
    for s in LATE:
        send_own(s)
    for copy in flags:
        copy.start()
    other_copies = {}
    for k in (n_ahead, n_peers):
        at_rows = slice((k // 2) * 2 * rows, (k // 2) * 2 * rows + 2 * rows)
        value = product((left_high[at_rows], left_low[at_rows]), both(total)) * weight
        panels(value[(k % 2) * rows:(k % 2 + 1) * rows], other_send, k)
        if k < n_peers:
            other_copies[k] = send(k, other_send, other_in, other_ssem, other_rsem, peers[k])
    for g in range(2):
        first = g * groups // 2
        near_copies[g].wait()
        solved_copies[g].wait()
        value = product(split(near_left[g]), both(solved_in[g])) * weight
        panels(value[:rows], other_in, first)
        panels(value[rows:], other_send, first + 1)
        for k in reversed(range(first + 1, first + n_ahead)):
            other_copies[k] = send(k, other_send, other_in, other_ssem, other_rsem, onward[k])

    def arrange(own_part, other_part, east, sender):
        for c in range(2):
            east_rows = jnp.broadcast_to(east[:1, :1], (rows, ext)) == 1
            a, b = own_part[c], other_part[c]
            out[c, sender, :, :ext] = jnp.where(east_rows, b, a)
            out[c, sender, :, ext:] = jnp.where(east_rows, a, b)

    arrange(own_send.at[n_peers], other_send.at[n_peers], flag[...], gy)
    for k in range(n_peers):
        flags[k].wait()
        own_copies[k].wait()
        if k in other_copies:
            other_copies[k].wait()
        arrange(own_in.at[k], other_in.at[k], flag_in[k], senders[k])


def on_device(gx_size, ring, near, iti, side, owner):
    width = iti.shape[-1]
    edge = width // 4
    ext = 3 * edge
    groups = ring * near
    rows = ext // groups
    span = (groups - near) // 2 * rows
    vmem, sems = pltpu.VMEM, DMA((groups,))
    iti, owner = (pltpu.with_memory_space_constraint(a, pltpu.HBM) for a in (iti, owner))
    out = pl.pallas_call(
        functools.partial(kernel, gx_size, ring, near),
        out_shape=jax.ShapeDtypeStruct((2, groups, rows, 2 * ext), f32),
        in_specs=[HBM, SMEM, HBM],
        out_specs=VMEM,
        scratch_shapes=[
            pltpu.SMEM((1, 1, groups), jnp.int32), vmem((2, ext, edge), f32), vmem((2, edge, width), f32),
            vmem((2, ext, ext), f32), vmem((ext, 2 * edge), f32),
            vmem((2, edge, edge), f32), vmem((2, edge, ext), f32),
            *[vmem((2 * edge, 2 * edge), bf16)] * 2, *[vmem((2 * edge, 2 * ext), bf16)] * 2,
            *[vmem((ext, 2 * edge), bf16)] * 2, vmem((1, 128), f32),
            vmem((2, span, 2 * edge), f32),
            *[vmem((groups, 2, rows, ext), f32)] * 4, vmem((groups, 1, 128), f32),
            *[vmem((LEVELS, edge, 2 * edge), bf16)] * 2, vmem((edge, 2 * ext), f32), vmem((2, edge, 2 * ext), f32),
            DMA((4,)), DMA, DMA, DMA((2,)), DMA((2,)), DMA, DMA, DMA((2,)), DMA((2,)), *[sems] * 6,
        ],
        compiler_params=pltpu.CompilerParams(
            collective_id=0, has_side_effects=True, vmem_limit_bytes=40 * 2**20
        ),
        name="merge",
    )(owner, side, iti)
    return out[None, None]


def solution(mesh):
    in_specs = (P("gx", "gy", None, None, None), P("gx", "gy"), P("gx", "gy", None))
    out_specs = P("gx", "gy", None, None, None, None)
    near = 2
    body = functools.partial(on_device, mesh.shape["gx"], mesh.shape["gy"] // near, near)
    return jax.shard_map(body, mesh=mesh, in_specs=in_specs, out_specs=out_specs, check_vma=False)
```

```python
import functools
import math

import jax
import jax.numpy as jnp
from jax import lax
from jax.experimental import pallas as pl
from jax.experimental.pallas import tpu as pltpu
from jax.sharding import PartitionSpec as P

SWEEPS = 15
LEVELS = (SWEEPS + 1).bit_length() - 1
MESH = pl.DeviceIdType.MESH
EARLY, LATE = (2, 1), (0, 3)
f32, bf16 = jnp.float32, jnp.bfloat16
VMEM, HBM, SMEM = (pl.BlockSpec(memory_space=m) for m in (pltpu.VMEM, pltpu.HBM, pltpu.SMEM))
DMA = pltpu.SemaphoreType.DMA


def split(x):
    high = x.astype(bf16)
    return high, (x - high.astype(f32)).astype(bf16)


def right_form(x):
    n = x.shape[1] // 2
    return jnp.concatenate([x, jnp.concatenate([-x[:, n:], x[:, :n]], axis=1)], axis=0)


def product(left, right):
    dot = functools.partial(jnp.dot, preferred_element_type=f32)
    return dot(left[0], right[0]) + (dot(left[0], right[1]) + dot(left[1], right[0]))


def both(x):
    high, low = split(x)
    return right_form(high), right_form(low)


def layout(ring, near):
    gy = lax.axis_index("gy")
    y, x = gy // near, lax.rem(gy, near)

    def index(s, t):
        return lax.rem(y + s + ring, ring) * near + lax.rem(x + t + near, near)

    half = ring // 2
    ahead = [(s, t) for s in range(1, half) for t in range(near)] + [(half, 0)]
    behind = [(-s, t) for s in range(1, half) for t in range(near)] + [(-half, 1)]
    places = ahead + [(0, 1)] + behind
    peers = [index(s, t) for s, t in places]
    senders = [index(-s, -t) for s, t in places]
    onward = [index(s - 1, t) for s, t in ahead] + [None] + [index(s + 1, t) for s, t in behind]
    return gy, peers, senders, onward, (index(1, 0), index(-1, 0)), len(ahead)


def sibling_of(gx_size):
    return lax.rem(lax.axis_index("gx") + gx_size // 2, gx_size), lax.axis_index("gy")


def kernel(
    gx_size, ring, near,
    owner, side, iti,
    out,
    owner_s, columns, edge_box, ext_box, left, qss, qse, edge_high, edge_low, ext_high, ext_low, left_high, left_low, flag, near_left,
    own_send, other_send, own_in, other_in, flag_in, powers_high, powers_low, solved, solved_in,
    load_sem, send_sem, recv_sem, near_ssem, near_rsem, edge_ssem, edge_rsem, solved_ssem, solved_rsem,
    own_ssem, own_rsem, other_ssem, other_rsem, flag_ssem, flag_rsem,
):
    edge = qss.shape[-1]
    ext = 3 * edge
    groups = ring * near
    rows = ext // groups
    loads = [
        pltpu.make_async_copy(owner, owner_s, load_sem.at[0]),
        pltpu.make_async_copy(iti.at[0, 0, :, :ext, ext:], columns, load_sem.at[1]),
        pltpu.make_async_copy(iti.at[0, 0, :, ext:, :], edge_box, load_sem.at[2]),
        pltpu.make_async_copy(iti.at[0, 0, :, :ext, :ext], ext_box, load_sem.at[3]),
    ]
    for load in loads:
        load.start()
    sibling = sibling_of(gx_size)
    gx = lax.axis_index("gx")
    gy, peers, senders, onward, neighbours, n_ahead = layout(ring, near)
    n_peers = len(peers)
    weight = math.sqrt(edge)
    barrier = pltpu.get_barrier_semaphore()
    pl.semaphore_signal(barrier, inc=1, device_id=sibling, device_id_type=MESH)
    for peer in reversed(peers):
        pl.semaphore_signal(barrier, inc=1, device_id=(gx, peer), device_id_type=MESH)
    pl.semaphore_wait(barrier, n_peers + 1)
    copy = pltpu.make_async_remote_copy(
        iti.at[0, 0, :, ext:, ext:], qss, send_sem, recv_sem, device_id=sibling, device_id_type=MESH
    )
    copy.start()

    loads[0].wait()
    loads[1].wait()
    owners = [owner_s[0, 0, p] for p in range(groups)]
    at = []
    for k, block in enumerate(peers + [gy]):
        panel = jnp.int32(0)
        for p in range(1, groups):
            panel = jnp.maximum(panel, (owners[p] == block).astype(jnp.int32) * p)
        at.append(panel * rows)
        for c in range(2):
            left[k * rows:(k + 1) * rows, c * edge:(c + 1) * edge] = columns[c, pl.ds(at[k], rows), :]
    span = n_ahead * rows
    near_copies = [
        pltpu.make_async_remote_copy(
            left.at[g * ext // 2:g * ext // 2 + span], near_left.at[g], near_ssem.at[g], near_rsem.at[g],
            device_id=(gx, neighbour), device_id_type=MESH,
        )
        for g, neighbour in enumerate(neighbours)
    ]
    for near_copy in near_copies:
        near_copy.start()
    left_high[...], left_low[...] = split(left[...])
    loads[2].wait()
    edge_rows = [edge_box[c] for c in range(2)]
    edge_high[...], edge_low[...] = both(jnp.concatenate([r[:, ext:] for r in edge_rows], axis=1))
    ext_high[...], ext_low[...] = both(jnp.concatenate([r[:, :ext] for r in edge_rows], axis=1))
    flag[...] = jnp.full(flag.shape, side[0, 0].astype(f32))
    copy.wait()
    se = pltpu.make_async_remote_copy(
        iti.at[0, 0, :, ext:, :ext], qse, edge_ssem, edge_rsem, device_id=sibling, device_id_type=MESH
    )
    se.start()
    q = split(jnp.concatenate([qss[0], qss[1]], axis=1))
    power = product(q, (edge_high[...], edge_low[...]))
    total = product(q, (ext_high[...], ext_low[...]))
    for level in range(LEVELS):
        high, low = split(power)
        powers_high[level] = high
        powers_low[level] = low
        total = total + product((high, low), both(total))
        if level + 1 < LEVELS:
            power = product((high, low), (right_form(high), right_form(low)))

    def panels(value, buffer, first, add=False):
        for m in range(value.shape[0] // rows):
            for c in range(2):
                piece = value[m * rows:(m + 1) * rows, c * ext:(c + 1) * ext]
                if add:
                    piece = ext_box[c, pl.ds(at[first + m], rows), :] * weight + piece
                buffer[first + m, c] = piece

    def send(k, buffer, into, ssem, rsem, peer):
        copy = pltpu.make_async_remote_copy(
            buffer.at[k], into.at[k], ssem.at[k], rsem.at[k], device_id=(gx, peer), device_id_type=MESH
        )
        copy.start()
        return copy

    own_copies = {}
    factor = both(total)

    pair = [[2 * s, 2 * s + 1, 2 * s + groups // 2, 2 * s + 1 + groups // 2] for s in range(4)]

    def own(s):
        for k in pair[s][::2]:
            at_rows = slice(k * rows, (k + 2) * rows)
            panels(product((left_high[at_rows], left_low[at_rows]), factor) * weight, own_send, k, add=True)

    def send_own(s):
        for k in (pair[s][0], pair[s][2], pair[s][1], pair[s][3]):
            if k < n_peers:
                own_copies[k] = send(k, own_send, own_in, own_ssem, own_rsem, peers[k])

    loads[3].wait()
    for s in EARLY:
        own(s)
        send_own(s)
    for s in LATE:
        own(s)
    flags = [
        pltpu.make_async_remote_copy(
            flag, flag_in.at[k], flag_ssem.at[k], flag_rsem.at[k], device_id=(gx, peer), device_id_type=MESH
        )
        for k, peer in enumerate(peers)
    ]
    se.wait()
    total = jnp.concatenate([qse[0], qse[1]], axis=1)
    for level in range(LEVELS):
        total = total + product((powers_high[level], powers_low[level]), both(total))
    solved[...] = total
    solved_copies = [
        pltpu.make_async_remote_copy(
            solved, solved_in.at[g], solved_ssem.at[g], solved_rsem.at[g], device_id=(gx, neighbour), device_id_type=MESH
        )
        for g, neighbour in enumerate(neighbours)
    ]
    for copy in solved_copies:
        copy.start()
    for s in LATE:
        send_own(s)
    for copy in flags:
        copy.start()
    other_copies = {}
    for k in (n_ahead, n_peers):
        at_rows = slice((k // 2) * 2 * rows, (k // 2) * 2 * rows + 2 * rows)
        value = product((left_high[at_rows], left_low[at_rows]), both(total)) * weight
        panels(value[(k % 2) * rows:(k % 2 + 1) * rows], other_send, k)
        if k < n_peers:
            other_copies[k] = send(k, other_send, other_in, other_ssem, other_rsem, peers[k])
    for g in range(2):
        first = g * groups // 2
        near_copies[g].wait()
        solved_copies[g].wait()
        value = product(split(near_left[g]), both(solved_in[g])) * weight
        panels(value[:rows], other_in, first)
        panels(value[rows:], other_send, first + 1)
        for k in reversed(range(first + 1, first + n_ahead)):
            other_copies[k] = send(k, other_send, other_in, other_ssem, other_rsem, onward[k])

    def arrange(own_part, other_part, east, sender):
        for c in range(2):
            east_rows = jnp.broadcast_to(east[:1, :1], (rows, ext)) == 1
            a, b = own_part[c], other_part[c]
            out[c, sender, :, :ext] = jnp.where(east_rows, b, a)
            out[c, sender, :, ext:] = jnp.where(east_rows, a, b)

    arrange(own_send.at[n_peers], other_send.at[n_peers], flag[...], gy)
    order = [n_ahead, 0, groups // 2]
    for g in range(2):
        order += reversed(range(g * groups // 2 + 1, g * groups // 2 + n_ahead))
    for k in order:
        flags[k].wait()
        own_copies[k].wait()
        if k in other_copies:
            other_copies[k].wait()
        arrange(own_in.at[k], other_in.at[k], flag_in[k], senders[k])


def on_device(gx_size, ring, near, iti, side, owner):
    width = iti.shape[-1]
    edge = width // 4
    ext = 3 * edge
    groups = ring * near
    rows = ext // groups
    span = (groups - near) // 2 * rows
    vmem, sems = pltpu.VMEM, DMA((groups,))
    iti, owner = (pltpu.with_memory_space_constraint(a, pltpu.HBM) for a in (iti, owner))
    out = pl.pallas_call(
        functools.partial(kernel, gx_size, ring, near),
        out_shape=jax.ShapeDtypeStruct((2, groups, rows, 2 * ext), f32),
        in_specs=[HBM, SMEM, HBM],
        out_specs=VMEM,
        scratch_shapes=[
            pltpu.SMEM((1, 1, groups), jnp.int32), vmem((2, ext, edge), f32), vmem((2, edge, width), f32),
            vmem((2, ext, ext), f32), vmem((ext, 2 * edge), f32),
            vmem((2, edge, edge), f32), vmem((2, edge, ext), f32),
            *[vmem((2 * edge, 2 * edge), bf16)] * 2, *[vmem((2 * edge, 2 * ext), bf16)] * 2,
            *[vmem((ext, 2 * edge), bf16)] * 2, vmem((1, 128), f32),
            vmem((2, span, 2 * edge), f32),
            *[vmem((groups, 2, rows, ext), f32)] * 4, vmem((groups, 1, 128), f32),
            *[vmem((LEVELS, edge, 2 * edge), bf16)] * 2, vmem((edge, 2 * ext), f32), vmem((2, edge, 2 * ext), f32),
            DMA((4,)), DMA, DMA, DMA((2,)), DMA((2,)), DMA, DMA, DMA((2,)), DMA((2,)), *[sems] * 6,
        ],
        compiler_params=pltpu.CompilerParams(
            collective_id=0, has_side_effects=True, vmem_limit_bytes=40 * 2**20
        ),
        name="merge",
    )(owner, side, iti)
    return out[None, None]


def solution(mesh):
    in_specs = (P("gx", "gy", None, None, None), P("gx", "gy"), P("gx", "gy", None))
    out_specs = P("gx", "gy", None, None, None, None)
    near = 2
    body = functools.partial(on_device, mesh.shape["gx"], mesh.shape["gy"] // near, near)
    return jax.shard_map(body, mesh=mesh, in_specs=in_specs, out_specs=out_specs, check_vma=False)
```
